32 devices in a mesh: groups: 2 (over y), seq: 4 (over x, core), head: 4 (over z).
Axes of the slice: x: 2, y: 2, z: 4, core: 2. Of those that a mesh axis runs over, the one named last changes fastest.
Arguments:
- queries: bfloat16 [2048, 64, 128], P(('groups', 'seq'), 'head'), parts along dimension 0, may hold values from -40 to 40
- seq_keys: bfloat16 [2048, 8, 128], P(('groups', 'seq'), 'head'), parts along dimension 0, may hold values from -6 to 6
- seq_values: bfloat16 [2048, 8, 128], P(('groups', 'seq'), 'head'), parts along dimension 0, may hold values from -6 to 6
- out_grad: bfloat16 [2048, 64, 128], P(('groups', 'seq'), 'head'), parts along dimension 0, may hold values from -6 to 6
- prefix_keys: bfloat16 [64, 8, 128], P(None, 'head'), may hold values from -6 to 6
- prefix_values: bfloat16 [64, 8, 128], P(None, 'head'), may hold values from -6 to 6
- global_ids: int32 [4], P('groups'), parts along dimension 0, may hold values from 0 to 7
- rand_owner: int32 [16, 2], P(('groups', 'seq')), parts along dimension 0, may hold values from 0 to 3, as said below
- rand_offset: int32 [16, 2], P(('groups', 'seq')), parts along dimension 0, may hold values from 0 to 1
- doc_length: int32 [2], P('groups'), parts along dimension 0, may hold values from 512 to 1024
Outputs:
- attn_out: bfloat16 [2048, 64, 128], P(('groups', 'seq'), 'head'), parts along dimension 0
- grad_queries: bfloat16 [2048, 64, 128], P(('groups', 'seq'), 'head'), parts along dimension 0
- grad_seq_keys: bfloat16 [2048, 8, 128], P(('groups', 'seq'), 'head'), parts along dimension 0
- grad_seq_values: bfloat16 [2048, 8, 128], P(('groups', 'seq'), 'head'), parts along dimension 0
- grad_prefix_keys: float32 [128, 8, 128], P('groups', 'head'), parts along dimension 0
- grad_prefix_values: float32 [128, 8, 128], P('groups', 'head'), parts along dimension 0
The draws below stay inside these ranges and needn't reach their ends.
There are 2 independent parts, one for each index of `groups`. The reference program is written for one: setup_inputs(seed, part) draws one part's arguments, and reference() takes and returns one part's arrays. A program takes and returns all parts, laid end to end along the dimension named above; an argument that names none is the same for every part. Nothing has to cross between parts.
Inputs may be any that keep to these rules, and one draw needn't show every extreme that they name: `rand_owner`: each row names 2 different indices; the 2 rows of one index of seq name any one index at most 2 times, and some index exactly 2 times.
All inputs are finite; a program needn't handle non-finite values.
Results may differ from the reference program's by a relative error of at most 0.0055.
Values may be sent and summed in bfloat16 or wider, within the bound.
A program may use at most 128 MiB of HBM per device.

```python
import math
import jax
import jax.numpy as jnp
from jax import lax

HEADS = 64
KVH = 8
HD = 128
BLK = 128
P_SIZE = 64
G = 2
R = 2
S_DEV = 256
SEQ = 1024
BPD = 2
NQB = 8
QPK = 8
CAP = 2
N_SEQ = 4


def draw_seq_keys(key, part):
    sampled = jnp.clip(jax.random.normal(jax.random.fold_in(key, 1), (SEQ, KVH, HD), jnp.float32), -6.0, 6.0)
    return sampled.astype(jnp.bfloat16)


def draw_queries(key, part):
    sampled = jnp.clip(jax.random.normal(jax.random.fold_in(key, 2), (SEQ, HEADS, HD), jnp.float32), -6.0, 6.0)
    return sampled.astype(jnp.bfloat16)


def draw_rand_owner(key, part):
    owner_keys = jax.random.split(jax.random.fold_in(key, 21), N_SEQ)
    orders = jax.vmap(lambda single: jax.random.permutation(single, N_SEQ))(owner_keys).astype(jnp.int32)
    shifts = jax.random.randint(jax.random.fold_in(key, 22), (N_SEQ,), 0, CAP).astype(jnp.int32)
    forced = jax.random.randint(jax.random.fold_in(key, 23), (), 0, N_SEQ).astype(jnp.int32)
    shifts = jnp.where(jnp.arange(N_SEQ, dtype=jnp.int32) == forced, 1, shifts).astype(jnp.int32)
    rows = jnp.arange(NQB, dtype=jnp.int32)
    device_of = rows // BPD
    within = rows % BPD
    slots = jnp.arange(R, dtype=jnp.int32)
    position = (within[:, None] + slots[None, :] * BPD + shifts[device_of][:, None]).astype(jnp.int32)
    bucket = (position % (N_SEQ * CAP) // CAP).astype(jnp.int32)
    return orders[device_of[:, None], bucket].astype(jnp.int32)


def touch_ends(array, rng, smallest, largest):
    index_at = [jax.random.randint(jax.random.fold_in(rng, axis), (), 0, length) for axis, length in enumerate(array.shape)]
    main_axis = array.shape.index(max(array.shape))
    next_to = index_at[:main_axis] + [(index_at[main_axis] + 1) % array.shape[main_axis]] + index_at[main_axis + 1:]
    return array.at[tuple(index_at)].set(smallest).at[tuple(next_to)].set(largest)


def levels(key, dims, cuts, low, top_value):
    def one(dim, parts):
        heights = jax.random.uniform(jax.random.fold_in(jax.random.fold_in(key, 6), dim), (parts,), jnp.float32, low / len(cuts), top_value / len(cuts))
        return jnp.repeat(jnp.exp(heights), dims[dim] // parts).reshape((-1,) + (1,) * (len(dims) - dim - 1))

    loudness = one(*cuts[0])
    for cut in cuts[1:]:
        loudness = loudness * one(*cut)
    return loudness


def gaussian(stream_key, dims, width, most, cuts=(), kind=jnp.bfloat16):
    loudness = levels(stream_key, dims, cuts, -0.22, 0.18) if cuts else 1.0
    array = jax.random.normal(stream_key, dims, jnp.float32) * width * loudness
    return jnp.minimum(jnp.maximum(array, -most), most).astype(kind)


def setup_inputs(seed: int = 0, part: int = 0) -> dict:
    streams_of = jax.random.split(jax.random.key(seed), 11)
    part_splits = jax.random.split(jax.random.fold_in(streams_of[10], part), 11)
    return {
        "queries": draw_queries(jax.random.fold_in(jax.random.fold_in(streams_of[10], part), 71), part),
        "seq_keys": draw_seq_keys(jax.random.fold_in(jax.random.fold_in(streams_of[10], part), 71), part),
        "seq_values": gaussian(part_splits[2], (SEQ, KVH, HD), 1.0, 6.0, ((0, 4), (1, 4))),
        "out_grad": gaussian(part_splits[3], (SEQ, HEADS, HD), 1.0, 6.0, ((0, 4), (1, 4))),
        "prefix_keys": gaussian(streams_of[4], (P_SIZE, KVH, HD), 1.0, 6.0, ((1, 4),)),
        "prefix_values": gaussian(streams_of[5], (P_SIZE, KVH, HD), 1.0, 6.0, ((1, 4),)),
        "global_ids": jax.random.randint(part_splits[6], (G,), 0, NQB).astype(jnp.int32),
        "rand_owner": draw_rand_owner(jax.random.fold_in(jax.random.fold_in(streams_of[10], part), 71), part),
        "rand_offset": touch_ends(jax.random.randint(part_splits[8], (NQB, R), 0, BPD), jax.random.fold_in(part_splits[8], 1), 0, BPD - 1).astype(jnp.int32),
        "doc_length": jax.random.randint(part_splits[9], (1,), SEQ // 2, SEQ + 1).astype(jnp.int32),
    }


masked_score = -1e+30

def block_list(query_rows, global_ids, rand_owner, rand_offset):
    count_rows = query_rows.shape[0]
    window = jnp.stack([query_rows - 1, query_rows], axis=1).astype(jnp.int32)
    globals_all = jnp.broadcast_to(global_ids[None, :], (count_rows, global_ids.shape[0])).astype(jnp.int32)
    randoms = (rand_owner * (S_DEV // BLK) + rand_offset).astype(jnp.int32)
    return jnp.concatenate([window, globals_all, randoms], axis=1)

def build_masks(query_rows, key_blocks, length):
    slot_count = key_blocks.shape[1]
    earlier_slot = jnp.arange(slot_count)[None, :] < jnp.arange(slot_count)[:, None]
    repeated = jnp.any((key_blocks[:, :, None] == key_blocks[:, None, :]) & earlier_slot[None], axis=2)
    allowed = (key_blocks >= 0) & (key_blocks <= query_rows[:, None]) & jnp.logical_not(repeated)
    within = jnp.arange(BLK, dtype=jnp.int32)
    key_pos = key_blocks[:, :, None] * BLK + within[None, None, :]
    query_pos = query_rows[:, None] * BLK + within[None, :]
    visible = allowed[:, None, :, None] & (key_pos[:, None] <= query_pos[:, :, None, None]) & (key_pos[:, None] < length)
    visible = visible.reshape(query_rows.shape[0], BLK, slot_count * BLK)
    prefix_cols = jnp.ones((query_rows.shape[0], BLK, P_SIZE), dtype=jnp.bool_)
    return (jnp.concatenate([prefix_cols, visible], axis=2), query_pos < length)

def attend(query_blk, grad_blk, key_rows, value_rows, visible, query_valid):
    scaling = 1.0 / math.sqrt(query_blk.shape[-1])
    query_f = query_blk.astype(jnp.float32)
    key_f = key_rows.astype(jnp.float32)
    value_f = value_rows.astype(jnp.float32)
    scores = jnp.einsum('tgqd,kgd->gqtk', query_f, key_f) * scaling
    scores = jnp.where(visible[None, None], scores, masked_score)
    maxima = lax.optimization_barrier(jnp.max(scores, axis=-1, keepdims=True))
    weights = jnp.where(visible[None, None], jnp.exp(scores - maxima), 0.0)
    probability = weights / lax.optimization_barrier(jnp.sum(weights, axis=-1, keepdims=True))
    prob_bf = probability.astype(jnp.bfloat16)
    valid_col = query_valid[:, None, None, None]
    mixed = jnp.einsum('gqtk,kgd->tgqd', prob_bf.astype(jnp.float32), value_f)
    attn_out = jnp.where(valid_col, mixed, 0.0).astype(jnp.bfloat16)
    masked_grad = jnp.where(valid_col, grad_blk, jnp.zeros_like(grad_blk))
    grad_f = masked_grad.astype(jnp.float32)
    grad_prob = jnp.einsum('tgqd,kgd->gqtk', grad_f, value_f)
    row_delta = lax.optimization_barrier(jnp.sum(probability * grad_prob, axis=-1, keepdims=True))
    grad_score = (probability * (grad_prob - row_delta)).astype(jnp.bfloat16)
    score_f = grad_score.astype(jnp.float32)
    grad_query = (scaling * jnp.einsum('gqtk,kgd->tgqd', score_f, key_f)).astype(jnp.bfloat16)
    grad_keys = scaling * jnp.einsum('gqtk,tgqd->kgd', score_f, query_f)
    grad_values = jnp.einsum('gqtk,tgqd->kgd', prob_bf.astype(jnp.float32), grad_f)
    return (attn_out, grad_query, grad_keys, grad_values)

def reference(queries, seq_keys, seq_values, out_grad, prefix_keys, prefix_values, global_ids, rand_owner, rand_offset, doc_length):
    total_len = queries.shape[0]
    blocks = total_len // BLK
    query_rows = jnp.arange(blocks, dtype=jnp.int32)
    key_blocks = block_list(query_rows, global_ids, rand_owner, rand_offset)
    visible_all, valid_all = build_masks(query_rows, key_blocks, doc_length[0])
    key_tiles = seq_keys.reshape(blocks, BLK, KVH, HD)
    value_tiles = seq_values.reshape(blocks, BLK, KVH, HD)
    query_tiles = queries.reshape(blocks, BLK, KVH, QPK, HD)
    grad_tiles = out_grad.reshape(blocks, BLK, KVH, QPK, HD)

    def scan_step(carried, block_item):
        acc_keys, acc_values, acc_pk, acc_pv = carried
        query_blk, grad_blk, listed, visible, query_valid = block_item
        safe_index = jnp.maximum(listed, 0).astype(jnp.int32)
        key_rows = jnp.concatenate([prefix_keys, key_tiles[safe_index].reshape(-1, KVH, HD)], axis=0)
        value_rows = jnp.concatenate([prefix_values, value_tiles[safe_index].reshape(-1, KVH, HD)], axis=0)
        attn_out, grad_query, grad_keys, grad_values = attend(query_blk, grad_blk, key_rows, value_rows, visible, query_valid)
        acc_keys = acc_keys.at[safe_index].add(grad_keys[P_SIZE:].reshape(-1, BLK, KVH, HD))
        acc_values = acc_values.at[safe_index].add(grad_values[P_SIZE:].reshape(-1, BLK, KVH, HD))
        acc_pk = acc_pk + grad_keys[:P_SIZE]
        acc_pv = acc_pv + grad_values[:P_SIZE]
        return ((acc_keys, acc_values, acc_pk, acc_pv), (attn_out, grad_query))
    initial = (jnp.zeros((blocks, BLK, KVH, HD), jnp.float32), jnp.zeros((blocks, BLK, KVH, HD), jnp.float32), jnp.zeros((P_SIZE, KVH, HD), jnp.float32), jnp.zeros((P_SIZE, KVH, HD), jnp.float32))
    finals, stacked = lax.scan(scan_step, initial, (query_tiles, grad_tiles, key_blocks, visible_all, valid_all))
    return (stacked[0].reshape(total_len, HEADS, HD), stacked[1].reshape(total_len, HEADS, HD), finals[0].reshape(total_len, KVH, HD).astype(jnp.bfloat16), finals[1].reshape(total_len, KVH, HD).astype(jnp.bfloat16), finals[2], finals[3])
```

```python
import functools
import math

import jax
import jax.numpy as jnp
from jax import lax
from jax.experimental import pallas as pl
from jax.experimental.pallas import tpu as pltpu
from jax.sharding import PartitionSpec as P

BLK = 128
LANES = 256
masked_score = -1e30


def dot(a, b, ca, cb):
    return lax.dot_general(a, b, (((ca,), (cb,)), ((), ())), preferred_element_type=jnp.float32)


def attend_kernel(
    per_dev, blocks, gids, owner, offset, length, q_ref, do_ref, kv_ref, pk_ref, pv_ref,
    o_ref, dq_ref, gkv_ref, gp_ref, k_s, v_s, p_s, ds_s, acc,
):
    b = pl.program_id(0)
    g = pl.program_id(1)
    last = (b == pl.num_programs(0) - 1) & (g == pl.num_programs(1) - 1)
    psz = pk_ref.shape[1]
    qheads, width = q_ref.shape[2], q_ref.shape[3]
    rows = BLK * qheads
    scaling = 1.0 / math.sqrt(width)
    i = lax.axis_index("seq") * per_dev + b
    doc = length[0]

    entries = [i - 1, i]
    entries += [gids[j] for j in range(gids.shape[0])]
    entries += [owner[b, j] * per_dev + offset[b, j] for j in range(owner.shape[1])]
    places, limits = [], []
    for j, e in enumerate(entries):
        ok = (e >= 0) & (e <= i)
        for earlier in entries[:j]:
            ok = ok & (e != earlier)
        places.append(jnp.where(ok, e, i))
        limits.append(jnp.where(ok, doc - e * BLK, 0))

    @pl.when((b == 0) & (g == 0))
    def _():
        acc[...] = jnp.zeros_like(acc)
        gp_ref[...] = jnp.zeros_like(gp_ref)

    k_s[0:psz, :] = pk_ref[g]
    v_s[0:psz, :] = pv_ref[g]
    for j, e in enumerate(places):
        at = pl.ds(psz + j * BLK, BLK)
        dev = e // per_dev
        inner = pl.ds(pl.multiple_of((e - dev * per_dev) * BLK, BLK), BLK)
        k_s[at, :] = kv_ref[dev, 0, g, inner, :]
        v_s[at, :] = kv_ref[dev, 1, g, inner, :]

    keys = k_s[...]
    values = v_s[...]
    keys_t = keys.T
    values_t = values.T
    step = LANES // qheads
    for c in range(rows // LANES):
        q = q_ref[c * step : (c + 1) * step, 0].reshape(LANES, width)
        row_t = i * BLK + c * step + lax.broadcasted_iota(jnp.int32, (LANES, width), 0) // qheads
        do = do_ref[c * step : (c + 1) * step, 0].reshape(LANES, width)
        do = jnp.where(row_t < doc, do.astype(jnp.float32), 0.0).astype(jnp.bfloat16)
        s = dot(keys, q, 1, 1) * (scaling * math.log2(math.e))
        key_at = lax.broadcasted_iota(jnp.int32, (BLK, LANES), 0)
        lane_t = c * step + lax.broadcasted_iota(jnp.int32, (BLK, LANES), 1) // qheads
        parts = [s[0:psz]]
        for j in range(len(places)):
            visible = key_at < limits[j]
            if j == 1:
                visible = visible & (key_at <= lane_t)
            parts.append(jnp.where(visible, s[psz + j * BLK : psz + (j + 1) * BLK], masked_score))
        s = jnp.concatenate(parts, axis=0)
        w = jnp.exp2(s - jnp.max(s, axis=0, keepdims=True))
        p = w * (1.0 / jnp.sum(w, axis=0, keepdims=True))
        p_bf = p.astype(jnp.bfloat16)
        p_s[:, c * LANES : (c + 1) * LANES] = p_bf
        dp = dot(values, do, 1, 1)
        delta = jnp.sum(p * dp, axis=0, keepdims=True)
        ds = (p * (dp - delta)).astype(jnp.bfloat16)
        ds_s[:, c * LANES : (c + 1) * LANES] = ds
        o = dot(values_t, p_bf, 1, 0).T
        o = jnp.where(row_t < doc, o, 0.0).astype(jnp.bfloat16)
        o_ref[c * step : (c + 1) * step, 0] = o.reshape(step, qheads, width)
        dq = (dot(keys_t, ds, 1, 0) * scaling).T.astype(jnp.bfloat16)
        dq_ref[c * step : (c + 1) * step, 0] = dq.reshape(step, qheads, width)

    all_t = i * BLK + lax.broadcasted_iota(jnp.int32, (rows, width), 0) // qheads
    do = do_ref[:, 0].reshape(rows, width)
    do = jnp.where(all_t < doc, do.astype(jnp.float32), 0.0).astype(jnp.bfloat16)
    gk = dot(ds_s[...], q_ref[:, 0].reshape(rows, width), 1, 0) * scaling
    gv = dot(p_s[...], do, 1, 0)
    for which, grad in ((0, gk), (1, gv)):
        gp_ref[which, g] += grad[0:psz]
        for j, e in enumerate(places):
            dev = e // per_dev
            inner = pl.ds(pl.multiple_of((e - dev * per_dev) * BLK, BLK), BLK)
            acc[dev, which, g, inner, :] += grad[psz + j * BLK : psz + (j + 1) * BLK]

    @pl.when(last)
    def _():
        gkv_ref[...] = acc[...].astype(gkv_ref.dtype)


def attend(q, do, kv, pk, pv, gids, owner, offset, length):
    tokens, groups, qheads, width = q.shape
    devices, per_tok = kv.shape[0], kv.shape[3]
    per_dev = tokens // BLK
    psz = pk.shape[1]
    total = psz + BLK * (2 + gids.shape[0] + owner.shape[1])
    tile = pl.BlockSpec((BLK, 1, qheads, width), lambda b, g: (b, g, 0, 0))
    smem = pl.BlockSpec(memory_space=pltpu.SMEM)
    vmem = pl.BlockSpec(memory_space=pltpu.VMEM)
    return pl.pallas_call(
        functools.partial(attend_kernel, per_dev, devices * per_dev),
        grid=(per_dev, groups),
        in_specs=[smem] * 4 + [tile, tile] + [vmem] * 3,
        out_specs=[tile, tile, vmem, vmem],
        out_shape=[
            jax.ShapeDtypeStruct(q.shape, jnp.bfloat16),
            jax.ShapeDtypeStruct(q.shape, jnp.bfloat16),
            jax.ShapeDtypeStruct(kv.shape, jnp.bfloat16),
            jax.ShapeDtypeStruct((2, groups, psz, width), jnp.float32),
        ],
        scratch_shapes=[
            pltpu.VMEM((total, width), jnp.bfloat16),
            pltpu.VMEM((total, width), jnp.bfloat16),
            pltpu.VMEM((total, BLK * qheads), jnp.bfloat16),
            pltpu.VMEM((total, BLK * qheads), jnp.bfloat16),
            pltpu.VMEM(kv.shape, jnp.float32),
        ],
        compiler_params=pltpu.CompilerParams(
            vmem_limit_bytes=50 * 2**20, dimension_semantics=("arbitrary", "arbitrary")
        ),
        cost_estimate=pl.CostEstimate(
            flops=10 * tokens * groups * qheads * total * width,
            bytes_accessed=8 * tokens * groups * qheads * width,
            transcendentals=tokens * groups * qheads * total,
        ),
    )(gids, owner, offset, length, q, do, kv, pk, pv)


def on_device(
    queries, seq_keys, seq_values, out_grad, prefix_keys, prefix_values,
    global_ids, rand_owner, rand_offset, doc_length,
):
    tokens, groups, width = seq_keys.shape
    shape = (tokens, groups, queries.shape[1] // groups, width)
    own = jnp.stack([seq_keys, seq_values]).transpose(0, 2, 1, 3)
    kv = lax.all_gather(own, "seq", axis=0)
    o, dq, gkv, gp = attend(
        queries.reshape(shape), out_grad.reshape(shape), kv,
        prefix_keys.transpose(1, 0, 2), prefix_values.transpose(1, 0, 2),
        global_ids, rand_owner, rand_offset, doc_length,
    )
    mine = lax.psum_scatter(gkv, "seq", scatter_dimension=0)
    gp = lax.psum(gp, "seq")
    mine = mine.astype(jnp.bfloat16).transpose(0, 2, 1, 3)
    gp = gp.transpose(0, 2, 1, 3)
    return (o.reshape(queries.shape), dq.reshape(queries.shape), mine[0], mine[1], gp[0], gp[1])


def solution(mesh):
    tok = P(("groups", "seq"), "head", None)
    pre = P(None, "head", None)
    row = P(("groups", "seq"), None)
    out = P("groups", "head", None)
    return jax.shard_map(
        on_device,
        mesh=mesh,
        in_specs=(tok, tok, tok, tok, pre, pre, P("groups"), row, row, P("groups")),
        out_specs=(tok, tok, tok, tok, out, out),
        check_vma=False,
    )
```

```python
import functools
import math

import jax
import jax.numpy as jnp
from jax import lax
from jax.experimental import pallas as pl
from jax.experimental.pallas import tpu as pltpu
from jax.sharding import PartitionSpec as P

BLK = 128
LANES = 256
MESH = pl.DeviceIdType.MESH
masked_score = -1e30


def dot(a, b, ca, cb):
    return lax.dot_general(a, b, (((ca,), (cb,)), ((), ())), preferred_element_type=jnp.float32)


def attend_kernel(
    per_dev, blocks, gids, owner, offset, length, q_ref, do_ref, kv_ref, pk_ref, pv_ref,
    o_ref, dq_ref, gkv_ref, gp_ref, k_s, v_s, p_s, ds_s, acc,
):
    b = pl.program_id(0)
    g = pl.program_id(1)
    last = (b == pl.num_programs(0) - 1) & (g == pl.num_programs(1) - 1)
    psz = pk_ref.shape[1]
    qheads, width = q_ref.shape[2], q_ref.shape[3]
    rows = BLK * qheads
    scaling = 1.0 / math.sqrt(width)
    i = lax.axis_index("seq") * per_dev + b
    doc = length[0]

    entries = [i - 1, i]
    entries += [gids[j] for j in range(gids.shape[0])]
    entries += [owner[b, j] * per_dev + offset[b, j] for j in range(owner.shape[1])]
    places, limits = [], []
    for j, e in enumerate(entries):
        ok = (e >= 0) & (e <= i)
        for earlier in entries[:j]:
            ok = ok & (e != earlier)
        places.append(jnp.where(ok, e, i))
        limits.append(jnp.where(ok, doc - e * BLK, 0))

    @pl.when((b == 0) & (g == 0))
    def _():
        acc[...] = jnp.zeros_like(acc)
        gp_ref[...] = jnp.zeros_like(gp_ref)

    k_s[0:psz, :] = pk_ref[g]
    v_s[0:psz, :] = pv_ref[g]
    for j, e in enumerate(places):
        at = pl.ds(psz + j * BLK, BLK)
        dev = e // per_dev
        inner = pl.ds(pl.multiple_of((e - dev * per_dev) * BLK, BLK), BLK)
        k_s[at, :] = kv_ref[dev, 0, g, inner, :]
        v_s[at, :] = kv_ref[dev, 1, g, inner, :]

    keys = k_s[...]
    values = v_s[...]
    keys_t = keys.T
    values_t = values.T
    step = LANES // qheads
    for c in range(rows // LANES):
        q = q_ref[c * step : (c + 1) * step, 0].reshape(LANES, width)
        row_t = i * BLK + c * step + lax.broadcasted_iota(jnp.int32, (LANES, width), 0) // qheads
        do = do_ref[c * step : (c + 1) * step, 0].reshape(LANES, width)
        do = jnp.where(row_t < doc, do.astype(jnp.float32), 0.0).astype(jnp.bfloat16)
        s = dot(keys, q, 1, 1) * (scaling * math.log2(math.e))
        key_at = lax.broadcasted_iota(jnp.int32, (BLK, LANES), 0)
        lane_t = c * step + lax.broadcasted_iota(jnp.int32, (BLK, LANES), 1) // qheads
        parts = [s[0:psz]]
        for j in range(len(places)):
            visible = key_at < limits[j]
            if j == 1:
                visible = visible & (key_at <= lane_t)
            parts.append(jnp.where(visible, s[psz + j * BLK : psz + (j + 1) * BLK], masked_score))
        s = jnp.concatenate(parts, axis=0)
        w = jnp.exp2(s - jnp.max(s, axis=0, keepdims=True))
        p = w * (1.0 / jnp.sum(w, axis=0, keepdims=True))
        p_bf = p.astype(jnp.bfloat16)
        p_s[:, c * LANES : (c + 1) * LANES] = p_bf
        dp = dot(values, do, 1, 1)
        delta = jnp.sum(p * dp, axis=0, keepdims=True)
        ds = (p * (dp - delta)).astype(jnp.bfloat16)
        ds_s[:, c * LANES : (c + 1) * LANES] = ds
        o = dot(values_t, p_bf, 1, 0).T
        o = jnp.where(row_t < doc, o, 0.0).astype(jnp.bfloat16)
        o_ref[c * step : (c + 1) * step, 0] = o.reshape(step, qheads, width)
        dq = (dot(keys_t, ds, 1, 0) * scaling).T.astype(jnp.bfloat16)
        dq_ref[c * step : (c + 1) * step, 0] = dq.reshape(step, qheads, width)

    all_t = i * BLK + lax.broadcasted_iota(jnp.int32, (rows, width), 0) // qheads
    do = do_ref[:, 0].reshape(rows, width)
    do = jnp.where(all_t < doc, do.astype(jnp.float32), 0.0).astype(jnp.bfloat16)
    gk = dot(ds_s[...], q_ref[:, 0].reshape(rows, width), 1, 0) * scaling
    gv = dot(p_s[...], do, 1, 0)
    for which, grad in ((0, gk), (1, gv)):
        gp_ref[which, g] += grad[0:psz]
        for j, e in enumerate(places):
            dev = e // per_dev
            inner = pl.ds(pl.multiple_of((e - dev * per_dev) * BLK, BLK), BLK)
            acc[dev, which, g, inner, :] += grad[psz + j * BLK : psz + (j + 1) * BLK]

    @pl.when(last)
    def _():
        gkv_ref[...] = acc[...].astype(gkv_ref.dtype)


def attend(q, do, kv, pk, pv, gids, owner, offset, length):
    tokens, groups, qheads, width = q.shape
    devices, per_tok = kv.shape[0], kv.shape[3]
    per_dev = tokens // BLK
    psz = pk.shape[1]
    total = psz + BLK * (2 + gids.shape[0] + owner.shape[1])
    tile = pl.BlockSpec((BLK, 1, qheads, width), lambda b, g: (b, g, 0, 0))
    smem = pl.BlockSpec(memory_space=pltpu.SMEM)
    vmem = pl.BlockSpec(memory_space=pltpu.VMEM)
    return pl.pallas_call(
        functools.partial(attend_kernel, per_dev, devices * per_dev),
        grid=(per_dev, groups),
        in_specs=[smem] * 4 + [tile, tile] + [vmem] * 3,
        out_specs=[tile, tile, vmem, vmem],
        out_shape=[
            jax.ShapeDtypeStruct(q.shape, jnp.bfloat16),
            jax.ShapeDtypeStruct(q.shape, jnp.bfloat16),
            jax.ShapeDtypeStruct(kv.shape, jnp.bfloat16),
            jax.ShapeDtypeStruct((2, groups, psz, width), jnp.float32),
        ],
        scratch_shapes=[
            pltpu.VMEM((total, width), jnp.bfloat16),
            pltpu.VMEM((total, width), jnp.bfloat16),
            pltpu.VMEM((total, BLK * qheads), jnp.bfloat16),
            pltpu.VMEM((total, BLK * qheads), jnp.bfloat16),
            pltpu.VMEM(kv.shape, jnp.float32),
        ],
        compiler_params=pltpu.CompilerParams(
            vmem_limit_bytes=50 * 2**20, dimension_semantics=("arbitrary", "arbitrary")
        ),
        cost_estimate=pl.CostEstimate(
            flops=10 * tokens * groups * qheads * total * width,
            bytes_accessed=8 * tokens * groups * qheads * width,
            transcendentals=tokens * groups * qheads * total,
        ),
    )(gids, owner, offset, length, q, do, kv, pk, pv)


def greet(n, me):
    barrier = pltpu.get_barrier_semaphore()
    for step in range(1, n):
        pl.semaphore_signal(
            barrier, inc=1, device_id={"seq": lax.rem(me + step, n)}, device_id_type=MESH
        )
    pl.semaphore_wait(barrier, n - 1)


def gather_kernel(n, own_ref, out_ref, send_sem, recv_sem):
    me = lax.axis_index("seq")
    chip, core = me // 2, me % 2
    chips = n // 2
    greet(n, me)

    def push(src, origin, to, slot):
        return pltpu.make_async_remote_copy(
            src_ref=src, dst_ref=out_ref.at[origin], send_sem=send_sem.at[slot],
            recv_sem=recv_sem.at[origin], device_id={"seq": to}, device_id_type=MESH,
        )

    for x in range(chips):
        @pl.when(x > chip)
        def _():
            push(own_ref, me, x * 2 + core, x).start()

    @pl.when(core == 0)
    def _():
        push(own_ref, me, me + 1, chips).start()

    out_ref[me] = own_ref[...]
    partner = chip * 2 + (1 - core)
    for x in range(chips):
        @pl.when(x < chip)
        def _():
            origin = x * 2 + core
            push(own_ref, origin, partner, x).wait_recv()
            push(out_ref.at[origin], origin, partner, x).start()

    for x in range(chips):
        @pl.when(x < chip)
        def _():
            push(own_ref, x * 2 + (1 - core), partner, x).wait_recv()
            push(out_ref.at[x * 2 + core], x * 2 + core, partner, x).wait_send()

        @pl.when(x > chip)
        def _():
            push(own_ref, me, x * 2 + core, x).wait_send()

    @pl.when(core == 0)
    def _():
        push(own_ref, me, me + 1, chips).wait_send()

    @pl.when(core == 1)
    def _():
        push(own_ref, me - 1, partner, chips).wait_recv()


def gather(own, n):
    vmem = pl.BlockSpec(memory_space=pltpu.VMEM)
    return pl.pallas_call(
        functools.partial(gather_kernel, n),
        in_specs=[vmem],
        out_specs=vmem,
        out_shape=jax.ShapeDtypeStruct((n,) + own.shape, own.dtype),
        scratch_shapes=[
            pltpu.SemaphoreType.DMA((n // 2 + 1,)),
            pltpu.SemaphoreType.DMA((n,)),
        ],
        compiler_params=pltpu.CompilerParams(
            collective_id=0, has_side_effects=True, vmem_limit_bytes=24 * 2**20
        ),
    )(own)


def reduce_kernel(
    n, g_ref, p_ref, k_out, v_out, p_out, near, far, sums, p_near, p_sum, p_far,
    near_send, near_recv, far_send, far_recv, p_send, p_recv, pf_send, pf_recv,
):
    me = lax.axis_index("seq")
    chip, core = me // 2, me % 2
    chips = n // 2
    partner = chip * 2 + (1 - core)
    greet(n, me)

    def move(src, dst, ss, rs, to):
        return pltpu.make_async_remote_copy(
            src_ref=src, dst_ref=dst, send_sem=ss, recv_sem=rs,
            device_id={"seq": to}, device_id_type=MESH,
        )

    def to_near(x):
        return move(g_ref.at[x * 2 + (1 - core)], near.at[x], near_send.at[x], near_recv.at[x], partner)

    def to_far(x):
        return move(sums.at[x], far.at[chip], far_send.at[x], far_recv.at[chip], x * 2 + core)

    def from_far(x):
        return move(sums.at[x], far.at[x], far_send.at[x], far_recv.at[x], x * 2 + core)

    def p_to_far(x):
        return move(p_sum, p_far.at[chip], pf_send.at[x], pf_recv.at[chip], x * 2 + core)

    def p_from_far(x):
        return move(p_sum, p_far.at[x], pf_send.at[x], pf_recv.at[x], x * 2 + core)

    p_first = move(p_ref.at[1 - core], p_near, p_send.at[0], p_recv.at[0], partner)
    p_first.start()
    for x in range(chips):
        @pl.when(x < chip)
        def _():
            to_near(x).start()

    @pl.when(core == 1)
    def _():
        to_near(chip).start()

    for x in range(chips):
        @pl.when(x < chip)
        def _():
            to_near(x).wait_recv()
            total = g_ref[x * 2 + core].astype(jnp.float32) + near[x].astype(jnp.float32)
            sums[x] = total.astype(sums.dtype)
            to_far(x).start()

    p_first.wait_recv()
    p_sum[...] = p_ref[core] + p_near[...]
    for x in range(chips):
        @pl.when(x != chip)
        def _():
            p_to_far(x).start()
    p_out[core] = p_sum[...]
    for x in range(chips):
        @pl.when(x != chip)
        def _():
            p_from_far(x).wait_recv()
            p_out[core] += p_far[x]
    p_mine = move(p_out.at[core], p_out.at[core], p_send.at[1], p_recv.at[1], partner)
    p_theirs = move(p_out.at[core], p_out.at[1 - core], p_send.at[1], p_recv.at[1], partner)
    p_mine.start()

    @pl.when(core == 0)
    def _():
        to_near(chip).wait_recv()
    for x in range(chips):
        @pl.when(x > chip)
        def _():
            from_far(x).wait_recv()

    for which, out in ((0, k_out), (1, v_out)):
        mine = g_ref[me, which].astype(jnp.float32)
        mine += jnp.where(core == 0, near[chip, which].astype(jnp.float32), 0.0)
        for x in range(1, chips):
            mine += jnp.where(x > chip, far[x, which].astype(jnp.float32), 0.0)
        out[...] = mine.astype(out.dtype)

    p_first.wait_send()
    for x in range(chips):
        @pl.when(x < chip)
        def _():
            to_near(x).wait_send()
            to_far(x).wait_send()

        @pl.when(x != chip)
        def _():
            p_to_far(x).wait_send()

    @pl.when(core == 1)
    def _():
        to_near(chip).wait_send()
    p_mine.wait_send()
    p_theirs.wait_recv()


def reduce(gkv, gp):
    n = gkv.shape[0]
    chips = n // 2
    vmem = pl.BlockSpec(memory_space=pltpu.VMEM)
    piece = gkv.shape[1:]
    dma = pltpu.SemaphoreType.DMA
    return pl.pallas_call(
        functools.partial(reduce_kernel, n),
        in_specs=[vmem] * 2,
        out_specs=[vmem] * 3,
        out_shape=[
            jax.ShapeDtypeStruct(piece[1:], gkv.dtype),
            jax.ShapeDtypeStruct(piece[1:], gkv.dtype),
            jax.ShapeDtypeStruct(gp.shape, gp.dtype),
        ],
        scratch_shapes=[
            pltpu.VMEM((chips,) + piece, gkv.dtype),
            pltpu.VMEM((chips,) + piece, gkv.dtype),
            pltpu.VMEM((chips,) + piece, gkv.dtype),
            pltpu.VMEM(gp.shape[1:], gp.dtype),
            pltpu.VMEM(gp.shape[1:], gp.dtype),
            pltpu.VMEM((chips,) + gp.shape[1:], gp.dtype),
            dma((chips,)), dma((chips,)), dma((chips,)), dma((chips,)),
            dma((2,)), dma((2,)), dma((chips,)), dma((chips,)),
        ],
        compiler_params=pltpu.CompilerParams(
            collective_id=1, has_side_effects=True, vmem_limit_bytes=32 * 2**20
        ),
    )(gkv, gp)


def on_device(
    queries, seq_keys, seq_values, out_grad, prefix_keys, prefix_values,
    global_ids, rand_owner, rand_offset, doc_length,
):
    tokens, groups, width = seq_keys.shape
    shape = (tokens, groups, queries.shape[1] // groups, width)
    own = jnp.stack([seq_keys, seq_values]).transpose(0, 2, 1, 3)
    kv = gather(own, lax.axis_size("seq"))
    o, dq, gkv, gp = attend(
        queries.reshape(shape), out_grad.reshape(shape), kv,
        prefix_keys.transpose(1, 0, 2), prefix_values.transpose(1, 0, 2),
        global_ids, rand_owner, rand_offset, doc_length,
    )
    gk, gv, gp = reduce(gkv, gp)
    gk, gv = gk.transpose(1, 0, 2), gv.transpose(1, 0, 2)
    gp = gp.transpose(0, 2, 1, 3)
    return (o.reshape(queries.shape), dq.reshape(queries.shape), gk, gv, gp[0], gp[1])


def solution(mesh):
    tok = P(("groups", "seq"), "head", None)
    pre = P(None, "head", None)
    row = P(("groups", "seq"), None)
    out = P("groups", "head", None)
    return jax.shard_map(
        on_device,
        mesh=mesh,
        in_specs=(tok, tok, tok, tok, pre, pre, P("groups"), row, row, P("groups")),
        out_specs=(tok, tok, tok, tok, out, out),
        check_vma=False,
    )
```

```python
import functools
import math

import jax
import jax.numpy as jnp
from jax import lax
from jax.experimental import pallas as pl
from jax.experimental.pallas import tpu as pltpu
from jax.sharding import PartitionSpec as P

BLK = 128
LANES = 1024
MESH = pl.DeviceIdType.MESH
masked_score = -1e30


def dot(a, b, ca, cb):
    return lax.dot_general(a, b, (((ca,), (cb,)), ((), ())), preferred_element_type=jnp.float32)


def attend_kernel(
    per_dev, blocks, gids, owner, offset, length, q_ref, do_ref, kv_ref, pk_ref, pv_ref,
    o_ref, dq_ref, gkv_ref, gp_ref, k_s, v_s, p_s, ds_s, acc,
):
    b = pl.program_id(0)
    g = pl.program_id(1)
    last = (b == pl.num_programs(0) - 1) & (g == pl.num_programs(1) - 1)
    psz = pk_ref.shape[1]
    qheads, width = q_ref.shape[2], q_ref.shape[3]
    rows = BLK * qheads
    scaling = 1.0 / math.sqrt(width)
    i = lax.axis_index("seq") * per_dev + b
    doc = length[0]

    entries = [i, i - 1]
    entries += [gids[j] for j in range(gids.shape[0])]
    entries += [owner[b, j] * per_dev + offset[b, j] for j in range(owner.shape[1])]
    slots = len(entries)
    places, count = [i] * slots, 0
    for j, e in enumerate(entries):
        ok = (e >= 0) & (e <= i) & (e * BLK < doc)
        for earlier in entries[:j]:
            ok = ok & (e != earlier)
        for k in range(j + 1):
            places[k] = jnp.where(ok & (count == k), e, places[k])
        count = count + ok.astype(jnp.int32)

    @pl.when((b == 0) & (g == 0))
    def _():
        acc[...] = jnp.zeros_like(acc)
        gp_ref[...] = jnp.zeros_like(gp_ref)

    def work(width_slots):
        total = psz + width_slots * BLK
        k_s[0:psz, :] = pk_ref[g]
        v_s[0:psz, :] = pv_ref[g]
        for j, e in enumerate(places[:width_slots]):
            at = pl.ds(psz + j * BLK, BLK)
            dev = e // per_dev
            inner = pl.ds(pl.multiple_of((e - dev * per_dev) * BLK, BLK), BLK)
            k_s[at, :] = kv_ref[dev, 0, g, inner, :]
            v_s[at, :] = kv_ref[dev, 1, g, inner, :]

        keys = k_s[0:total, :]
        values = v_s[0:total, :]
        keys_t = keys.T
        values_t = values.T
        step = LANES // qheads
        for c in range(rows // LANES):
            q = q_ref[c * step : (c + 1) * step, 0].reshape(LANES, width)
            row_t = i * BLK + c * step + lax.broadcasted_iota(jnp.int32, (LANES, width), 0) // qheads
            do = do_ref[c * step : (c + 1) * step, 0].reshape(LANES, width)
            do = jnp.where(row_t < doc, do.astype(jnp.float32), 0.0).astype(jnp.bfloat16)
            s = dot(keys, q, 1, 1) * (scaling * math.log2(math.e))
            key_at = lax.broadcasted_iota(jnp.int32, (BLK, LANES), 0)
            lane_t = c * step + lax.broadcasted_iota(jnp.int32, (BLK, LANES), 1) // qheads
            parts = [s[0:psz]]
            for j in range(width_slots):
                visible = key_at < jnp.where(j < count, doc - places[j] * BLK, 0)
                if j == 0:
                    visible = visible & (key_at <= lane_t)
                parts.append(jnp.where(visible, s[psz + j * BLK : psz + (j + 1) * BLK], masked_score))
            s = jnp.concatenate(parts, axis=0)
            w = jnp.exp2(s - jnp.max(s, axis=0, keepdims=True))
            p = w * (1.0 / jnp.sum(w, axis=0, keepdims=True))
            p_bf = p.astype(jnp.bfloat16)
            p_s[0:total, c * LANES : (c + 1) * LANES] = p_bf
            dp = dot(values, do, 1, 1)
            delta = jnp.sum(p * dp, axis=0, keepdims=True)
            ds = (p * (dp - delta)).astype(jnp.bfloat16)
            ds_s[0:total, c * LANES : (c + 1) * LANES] = ds
            o = dot(values_t, p_bf, 1, 0).T
            o = jnp.where(row_t < doc, o, 0.0).astype(jnp.bfloat16)
            o_ref[c * step : (c + 1) * step, 0] = o.reshape(step, qheads, width)
            dq = (dot(keys_t, ds, 1, 0) * scaling).T.astype(jnp.bfloat16)
            dq_ref[c * step : (c + 1) * step, 0] = dq.reshape(step, qheads, width)

        all_t = i * BLK + lax.broadcasted_iota(jnp.int32, (rows, width), 0) // qheads
        do = do_ref[:, 0].reshape(rows, width)
        do = jnp.where(all_t < doc, do.astype(jnp.float32), 0.0).astype(jnp.bfloat16)
        gk = dot(ds_s[0:total, :], q_ref[:, 0].reshape(rows, width), 1, 0) * scaling
        gv = dot(p_s[0:total, :], do, 1, 0)
        for which, grad in ((0, gk), (1, gv)):
            gp_ref[which, g] += grad[0:psz]
            for j, e in enumerate(places[:width_slots]):
                dev = e // per_dev
                inner = pl.ds(pl.multiple_of((e - dev * per_dev) * BLK, BLK), BLK)
                acc[dev, which, g, inner, :] += grad[psz + j * BLK : psz + (j + 1) * BLK]

    fewest = 2
    for m in range(fewest, slots + 1):
        fits = (count == m) if m > fewest else (count <= m)

        @pl.when((i * BLK < doc) & fits)
        def _():
            work(m)

    @pl.when(i * BLK >= doc)
    def _():
        o_ref[...] = jnp.zeros_like(o_ref)
        dq_ref[...] = jnp.zeros_like(dq_ref)

    @pl.when(last)
    def _():
        gkv_ref[...] = acc[...].astype(gkv_ref.dtype)


def attend(q, do, kv, pk, pv, gids, owner, offset, length):
    tokens, groups, qheads, width = q.shape
    devices, per_tok = kv.shape[0], kv.shape[3]
    per_dev = tokens // BLK
    psz = pk.shape[1]
    total = psz + BLK * (2 + gids.shape[0] + owner.shape[1])
    tile = pl.BlockSpec((BLK, 1, qheads, width), lambda b, g: (b, g, 0, 0))
    smem = pl.BlockSpec(memory_space=pltpu.SMEM)
    vmem = pl.BlockSpec(memory_space=pltpu.VMEM)
    return pl.pallas_call(
        functools.partial(attend_kernel, per_dev, devices * per_dev),
        grid=(per_dev, groups),
        in_specs=[smem] * 4 + [tile, tile] + [vmem] * 3,
        out_specs=[tile, tile, vmem, vmem],
        out_shape=[
            jax.ShapeDtypeStruct(q.shape, jnp.bfloat16),
            jax.ShapeDtypeStruct(q.shape, jnp.bfloat16),
            jax.ShapeDtypeStruct(kv.shape, jnp.bfloat16),
            jax.ShapeDtypeStruct((2, groups, psz, width), jnp.float32),
        ],
        scratch_shapes=[
            pltpu.VMEM((total, width), jnp.bfloat16),
            pltpu.VMEM((total, width), jnp.bfloat16),
            pltpu.VMEM((total, BLK * qheads), jnp.bfloat16),
            pltpu.VMEM((total, BLK * qheads), jnp.bfloat16),
            pltpu.VMEM(kv.shape, jnp.float32),
        ],
        compiler_params=pltpu.CompilerParams(
            vmem_limit_bytes=50 * 2**20, dimension_semantics=("arbitrary", "arbitrary")
        ),
        cost_estimate=pl.CostEstimate(
            flops=10 * tokens * groups * qheads * total * width,
            bytes_accessed=8 * tokens * groups * qheads * width,
            transcendentals=tokens * groups * qheads * total,
        ),
    )(gids, owner, offset, length, q, do, kv, pk, pv)


def greet(n, me):
    barrier = pltpu.get_barrier_semaphore()
    for step in range(1, n):
        pl.semaphore_signal(
            barrier, inc=1, device_id={"seq": lax.rem(me + step, n)}, device_id_type=MESH
        )
    pl.semaphore_wait(barrier, n - 1)


def gather_kernel(n, own_ref, out_ref, send_sem, recv_sem):
    me = lax.axis_index("seq")
    chip, core = me // 2, me % 2
    chips = n // 2
    greet(n, me)

    def push(src, origin, to, slot):
        return pltpu.make_async_remote_copy(
            src_ref=src, dst_ref=out_ref.at[origin], send_sem=send_sem.at[slot],
            recv_sem=recv_sem.at[origin], device_id={"seq": to}, device_id_type=MESH,
        )

    for x in range(chips):
        @pl.when(x > chip)
        def _():
            push(own_ref, me, x * 2 + core, x).start()

    @pl.when(core == 0)
    def _():
        push(own_ref, me, me + 1, chips).start()

    out_ref[me] = own_ref[...]
    partner = chip * 2 + (1 - core)
    for x in range(chips):
        @pl.when(x < chip)
        def _():
            origin = x * 2 + core
            push(own_ref, origin, partner, x).wait_recv()
            push(out_ref.at[origin], origin, partner, x).start()

    for x in range(chips):
        @pl.when(x < chip)
        def _():
            push(own_ref, x * 2 + (1 - core), partner, x).wait_recv()
            push(out_ref.at[x * 2 + core], x * 2 + core, partner, x).wait_send()

        @pl.when(x > chip)
        def _():
            push(own_ref, me, x * 2 + core, x).wait_send()

    @pl.when(core == 0)
    def _():
        push(own_ref, me, me + 1, chips).wait_send()

    @pl.when(core == 1)
    def _():
        push(own_ref, me - 1, partner, chips).wait_recv()


def gather(own, n):
    vmem = pl.BlockSpec(memory_space=pltpu.VMEM)
    return pl.pallas_call(
        functools.partial(gather_kernel, n),
        in_specs=[vmem],
        out_specs=vmem,
        out_shape=jax.ShapeDtypeStruct((n,) + own.shape, own.dtype),
        scratch_shapes=[
            pltpu.SemaphoreType.DMA((n // 2 + 1,)),
            pltpu.SemaphoreType.DMA((n,)),
        ],
        compiler_params=pltpu.CompilerParams(
            collective_id=0, has_side_effects=True, vmem_limit_bytes=24 * 2**20
        ),
    )(own)


def reduce_kernel(
    n, g_ref, p_ref, k_out, v_out, p_out, near, far, sums, p_near, p_sum, p_far,
    near_send, near_recv, far_send, far_recv, p_send, p_recv, pf_send, pf_recv,
):
    me = lax.axis_index("seq")
    chip, core = me // 2, me % 2
    chips = n // 2
    partner = chip * 2 + (1 - core)
    greet(n, me)

    def move(src, dst, ss, rs, to):
        return pltpu.make_async_remote_copy(
            src_ref=src, dst_ref=dst, send_sem=ss, recv_sem=rs,
            device_id={"seq": to}, device_id_type=MESH,
        )

    def to_near(x):
        return move(g_ref.at[x * 2 + (1 - core)], near.at[x], near_send.at[x], near_recv.at[x], partner)

    def to_far(x):
        return move(sums.at[x], far.at[chip], far_send.at[x], far_recv.at[chip], x * 2 + core)

    def from_far(x):
        return move(sums.at[x], far.at[x], far_send.at[x], far_recv.at[x], x * 2 + core)

    def p_to_far(x):
        return move(p_sum, p_far.at[chip], pf_send.at[x], pf_recv.at[chip], x * 2 + core)

    def p_from_far(x):
        return move(p_sum, p_far.at[x], pf_send.at[x], pf_recv.at[x], x * 2 + core)

    p_first = move(p_ref.at[1 - core], p_near, p_send.at[0], p_recv.at[0], partner)
    p_first.start()
    for x in range(chips):
        @pl.when(x < chip)
        def _():
            to_near(x).start()

    @pl.when(core == 1)
    def _():
        to_near(chip).start()

    for x in range(chips):
        @pl.when(x < chip)
        def _():
            to_near(x).wait_recv()
            total = g_ref[x * 2 + core].astype(jnp.float32) + near[x].astype(jnp.float32)
            sums[x] = total.astype(sums.dtype)
            to_far(x).start()

    p_first.wait_recv()
    p_sum[...] = p_ref[core] + p_near[...]
    for x in range(chips):
        @pl.when(x != chip)
        def _():
            p_to_far(x).start()
    p_out[core] = p_sum[...]
    for x in range(chips):
        @pl.when(x != chip)
        def _():
            p_from_far(x).wait_recv()
            p_out[core] += p_far[x]
    p_mine = move(p_out.at[core], p_out.at[core], p_send.at[1], p_recv.at[1], partner)
    p_theirs = move(p_out.at[core], p_out.at[1 - core], p_send.at[1], p_recv.at[1], partner)
    p_mine.start()

    @pl.when(core == 0)
    def _():
        to_near(chip).wait_recv()
    for x in range(chips):
        @pl.when(x > chip)
        def _():
            from_far(x).wait_recv()

    for which, out in ((0, k_out), (1, v_out)):
        mine = g_ref[me, which].astype(jnp.float32)
        mine += jnp.where(core == 0, near[chip, which].astype(jnp.float32), 0.0)
        for x in range(1, chips):
            mine += jnp.where(x > chip, far[x, which].astype(jnp.float32), 0.0)
        out[...] = mine.astype(out.dtype)

    p_first.wait_send()
    for x in range(chips):
        @pl.when(x < chip)
        def _():
            to_near(x).wait_send()
            to_far(x).wait_send()

        @pl.when(x != chip)
        def _():
            p_to_far(x).wait_send()

    @pl.when(core == 1)
    def _():
        to_near(chip).wait_send()
    p_mine.wait_send()
    p_theirs.wait_recv()


def reduce(gkv, gp):
    n = gkv.shape[0]
    chips = n // 2
    vmem = pl.BlockSpec(memory_space=pltpu.VMEM)
    piece = gkv.shape[1:]
    dma = pltpu.SemaphoreType.DMA
    return pl.pallas_call(
        functools.partial(reduce_kernel, n),
        in_specs=[vmem] * 2,
        out_specs=[vmem] * 3,
        out_shape=[
            jax.ShapeDtypeStruct(piece[1:], gkv.dtype),
            jax.ShapeDtypeStruct(piece[1:], gkv.dtype),
            jax.ShapeDtypeStruct(gp.shape, gp.dtype),
        ],
        scratch_shapes=[
            pltpu.VMEM((chips,) + piece, gkv.dtype),
            pltpu.VMEM((chips,) + piece, gkv.dtype),
            pltpu.VMEM((chips,) + piece, gkv.dtype),
            pltpu.VMEM(gp.shape[1:], gp.dtype),
            pltpu.VMEM(gp.shape[1:], gp.dtype),
            pltpu.VMEM((chips,) + gp.shape[1:], gp.dtype),
            dma((chips,)), dma((chips,)), dma((chips,)), dma((chips,)),
            dma((2,)), dma((2,)), dma((chips,)), dma((chips,)),
        ],
        compiler_params=pltpu.CompilerParams(
            collective_id=1, has_side_effects=True, vmem_limit_bytes=32 * 2**20
        ),
    )(gkv, gp)


def on_device(
    queries, seq_keys, seq_values, out_grad, prefix_keys, prefix_values,
    global_ids, rand_owner, rand_offset, doc_length,
):
    tokens, groups, width = seq_keys.shape
    shape = (tokens, groups, queries.shape[1] // groups, width)
    own = jnp.stack([seq_keys, seq_values]).transpose(0, 2, 1, 3)
    kv = gather(own, lax.axis_size("seq"))
    o, dq, gkv, gp = attend(
        queries.reshape(shape), out_grad.reshape(shape), kv,
        prefix_keys.transpose(1, 0, 2), prefix_values.transpose(1, 0, 2),
        global_ids, rand_owner, rand_offset, doc_length,
    )
    gk, gv, gp = reduce(gkv, gp)
    gk, gv = gk.transpose(1, 0, 2), gv.transpose(1, 0, 2)
    gp = gp.transpose(0, 2, 1, 3)
    return (o.reshape(queries.shape), dq.reshape(queries.shape), gk, gv, gp[0], gp[1])


def solution(mesh):
    tok = P(("groups", "seq"), "head", None)
    pre = P(None, "head", None)
    row = P(("groups", "seq"), None)
    out = P("groups", "head", None)
    return jax.shard_map(
        on_device,
        mesh=mesh,
        in_specs=(tok, tok, tok, tok, pre, pre, P("groups"), row, row, P("groups")),
        out_specs=(tok, tok, tok, tok, out, out),
        check_vma=False,
    )
```

```python
import functools
import math

import jax
import jax.numpy as jnp
from jax import lax
from jax.experimental import pallas as pl
from jax.experimental.pallas import tpu as pltpu
from jax.sharding import PartitionSpec as P

BLK = 128
LANES = 1024
MESH = pl.DeviceIdType.MESH
masked_score = -1e30


def dot(a, b, ca, cb):
    return lax.dot_general(a, b, (((ca,), (cb,)), ((), ())), preferred_element_type=jnp.float32)


def attend_kernel(
    per_dev, blocks, gids, owner, offset, length, q_ref, do_ref, kv_ref, pk_ref, pv_ref,
    o_ref, dq_ref, gkv_ref, gp_ref, k_s, v_s, acc,
):
    b = pl.program_id(0)
    g = pl.program_id(1)
    last = (b == pl.num_programs(0) - 1) & (g == pl.num_programs(1) - 1)
    psz = pk_ref.shape[1]
    qheads, width = q_ref.shape[2], q_ref.shape[3]
    rows = BLK * qheads
    scaling = 1.0 / math.sqrt(width)
    i = lax.axis_index("seq") * per_dev + b
    doc = length[0]

    entries = [i, i - 1]
    entries += [gids[j] for j in range(gids.shape[0])]
    entries += [owner[b, j] * per_dev + offset[b, j] for j in range(owner.shape[1])]
    slots = len(entries)
    places, count = [i] * slots, 0
    for j, e in enumerate(entries):
        ok = (e >= 0) & (e <= i) & (e * BLK < doc)
        for earlier in entries[:j]:
            ok = ok & (e != earlier)
        for k in range(j + 1):
            places[k] = jnp.where(ok & (count == k), e, places[k])
        count = count + ok.astype(jnp.int32)

    @pl.when((b == 0) & (g == 0))
    def _():
        acc[...] = jnp.zeros_like(acc)
        gp_ref[...] = jnp.zeros_like(gp_ref)

    def work(width_slots):
        total = psz + width_slots * BLK
        k_s[0:psz, :] = pk_ref[g]
        v_s[0:psz, :] = pv_ref[g]
        for j, e in enumerate(places[:width_slots]):
            at = pl.ds(psz + j * BLK, BLK)
            dev = e // per_dev
            inner = pl.ds(pl.multiple_of((e - dev * per_dev) * BLK, BLK), BLK)
            k_s[at, :] = kv_ref[dev, 0, g, inner, :]
            v_s[at, :] = kv_ref[dev, 1, g, inner, :]

        keys = k_s[0:total, :]
        values = v_s[0:total, :]
        keys_t = keys.T
        values_t = values.T
        step = LANES // qheads
        gk = gv = 0.0
        for c in range(rows // LANES):
            q = q_ref[c * step : (c + 1) * step, 0].reshape(LANES, width)
            row_t = i * BLK + c * step + lax.broadcasted_iota(jnp.int32, (LANES, width), 0) // qheads
            do = do_ref[c * step : (c + 1) * step, 0].reshape(LANES, width)
            do = jnp.where(row_t < doc, do.astype(jnp.float32), 0.0).astype(jnp.bfloat16)
            s = dot(keys, q, 1, 1) * (scaling * math.log2(math.e))
            key_at = lax.broadcasted_iota(jnp.int32, (BLK, LANES), 0)
            lane_t = c * step + lax.broadcasted_iota(jnp.int32, (BLK, LANES), 1) // qheads
            parts = [s[0:psz]]
            for j in range(width_slots):
                visible = key_at < jnp.where(j < count, doc - places[j] * BLK, 0)
                if j == 0:
                    visible = visible & (key_at <= lane_t)
                parts.append(jnp.where(visible, s[psz + j * BLK : psz + (j + 1) * BLK], masked_score))
            s = jnp.concatenate(parts, axis=0)
            w = jnp.exp2(s - jnp.max(s, axis=0, keepdims=True))
            p = w * (1.0 / jnp.sum(w, axis=0, keepdims=True))
            p_bf = p.astype(jnp.bfloat16)
            gv = gv + dot(p_bf, do, 1, 0)
            dp = dot(values, do, 1, 1)
            delta = jnp.sum(p * dp, axis=0, keepdims=True)
            ds = (p * (dp - delta)).astype(jnp.bfloat16)
            gk = gk + dot(ds, q, 1, 0)
            o = dot(values_t, p_bf, 1, 0).T
            o = jnp.where(row_t < doc, o, 0.0).astype(jnp.bfloat16)
            o_ref[c * step : (c + 1) * step, 0] = o.reshape(step, qheads, width)
            dq = (dot(keys_t, ds, 1, 0) * scaling).T.astype(jnp.bfloat16)
            dq_ref[c * step : (c + 1) * step, 0] = dq.reshape(step, qheads, width)

        gk = gk * scaling
        for which, grad in ((0, gk), (1, gv)):
            gp_ref[which, g] += grad[0:psz]
            for j, e in enumerate(places[:width_slots]):
                dev = e // per_dev
                inner = pl.ds(pl.multiple_of((e - dev * per_dev) * BLK, BLK), BLK)
                acc[dev, which, g, inner, :] += grad[psz + j * BLK : psz + (j + 1) * BLK]

    fewest = 2
    for m in range(fewest, slots + 1):
        fits = (count == m) if m > fewest else (count <= m)

        @pl.when((i * BLK < doc) & fits)
        def _():
            work(m)

    @pl.when(i * BLK >= doc)
    def _():
        o_ref[...] = jnp.zeros_like(o_ref)
        dq_ref[...] = jnp.zeros_like(dq_ref)

    @pl.when(last)
    def _():
        gkv_ref[...] = acc[...].astype(gkv_ref.dtype)


def attend(q, do, kv, pk, pv, gids, owner, offset, length):
    tokens, groups, qheads, width = q.shape
    devices, per_tok = kv.shape[0], kv.shape[3]
    per_dev = tokens // BLK
    psz = pk.shape[1]
    total = psz + BLK * (2 + gids.shape[0] + owner.shape[1])
    tile = pl.BlockSpec((BLK, 1, qheads, width), lambda b, g: (b, g, 0, 0))
    smem = pl.BlockSpec(memory_space=pltpu.SMEM)
    vmem = pl.BlockSpec(memory_space=pltpu.VMEM)
    return pl.pallas_call(
        functools.partial(attend_kernel, per_dev, devices * per_dev),
        grid=(per_dev, groups),
        in_specs=[smem] * 4 + [tile, tile] + [vmem] * 3,
        out_specs=[tile, tile, vmem, vmem],
        out_shape=[
            jax.ShapeDtypeStruct(q.shape, jnp.bfloat16),
            jax.ShapeDtypeStruct(q.shape, jnp.bfloat16),
            jax.ShapeDtypeStruct(kv.shape, jnp.bfloat16),
            jax.ShapeDtypeStruct((2, groups, psz, width), jnp.float32),
        ],
        scratch_shapes=[
            pltpu.VMEM((total, width), jnp.bfloat16),
            pltpu.VMEM((total, width), jnp.bfloat16),
            pltpu.VMEM(kv.shape, jnp.float32),
        ],
        compiler_params=pltpu.CompilerParams(
            vmem_limit_bytes=50 * 2**20, dimension_semantics=("arbitrary", "arbitrary")
        ),
        cost_estimate=pl.CostEstimate(
            flops=10 * tokens * groups * qheads * total * width,
            bytes_accessed=8 * tokens * groups * qheads * width,
            transcendentals=tokens * groups * qheads * total,
        ),
    )(gids, owner, offset, length, q, do, kv, pk, pv)


def greet(n, me):
    barrier = pltpu.get_barrier_semaphore()
    for step in range(1, n):
        pl.semaphore_signal(
            barrier, inc=1, device_id={"seq": lax.rem(me + step, n)}, device_id_type=MESH
        )
    pl.semaphore_wait(barrier, n - 1)


def gather_kernel(n, own_ref, out_ref, send_sem, recv_sem):
    me = lax.axis_index("seq")
    chip, core = me // 2, me % 2
    chips = n // 2
    greet(n, me)

    def push(src, origin, to, slot):
        return pltpu.make_async_remote_copy(
            src_ref=src, dst_ref=out_ref.at[origin], send_sem=send_sem.at[slot],
            recv_sem=recv_sem.at[origin], device_id={"seq": to}, device_id_type=MESH,
        )

    for x in range(chips):
        @pl.when(x > chip)
        def _():
            push(own_ref, me, x * 2 + core, x).start()

    @pl.when(core == 0)
    def _():
        push(own_ref, me, me + 1, chips).start()

    out_ref[me] = own_ref[...]
    partner = chip * 2 + (1 - core)
    for x in range(chips):
        @pl.when(x < chip)
        def _():
            origin = x * 2 + core
            push(own_ref, origin, partner, x).wait_recv()
            push(out_ref.at[origin], origin, partner, x).start()

    for x in range(chips):
        @pl.when(x < chip)
        def _():
            push(own_ref, x * 2 + (1 - core), partner, x).wait_recv()
            push(out_ref.at[x * 2 + core], x * 2 + core, partner, x).wait_send()

        @pl.when(x > chip)
        def _():
            push(own_ref, me, x * 2 + core, x).wait_send()

    @pl.when(core == 0)
    def _():
        push(own_ref, me, me + 1, chips).wait_send()

    @pl.when(core == 1)
    def _():
        push(own_ref, me - 1, partner, chips).wait_recv()


def gather(own, n):
    vmem = pl.BlockSpec(memory_space=pltpu.VMEM)
    return pl.pallas_call(
        functools.partial(gather_kernel, n),
        in_specs=[vmem],
        out_specs=vmem,
        out_shape=jax.ShapeDtypeStruct((n,) + own.shape, own.dtype),
        scratch_shapes=[
            pltpu.SemaphoreType.DMA((n // 2 + 1,)),
            pltpu.SemaphoreType.DMA((n,)),
        ],
        compiler_params=pltpu.CompilerParams(
            collective_id=0, has_side_effects=True, vmem_limit_bytes=24 * 2**20
        ),
    )(own)


def reduce_kernel(
    n, g_ref, p_ref, k_out, v_out, p_out, near, far, sums, p_near, p_sum, p_far,
    near_send, near_recv, far_send, far_recv, p_send, p_recv, pf_send, pf_recv,
):
    me = lax.axis_index("seq")
    chip, core = me // 2, me % 2
    chips = n // 2
    partner = chip * 2 + (1 - core)
    greet(n, me)

    def move(src, dst, ss, rs, to):
        return pltpu.make_async_remote_copy(
            src_ref=src, dst_ref=dst, send_sem=ss, recv_sem=rs,
            device_id={"seq": to}, device_id_type=MESH,
        )

    def to_near(x):
        return move(g_ref.at[x * 2 + (1 - core)], near.at[x], near_send.at[x], near_recv.at[x], partner)

    def to_far(x):
        return move(sums.at[x], far.at[chip], far_send.at[x], far_recv.at[chip], x * 2 + core)

    def from_far(x):
        return move(sums.at[x], far.at[x], far_send.at[x], far_recv.at[x], x * 2 + core)

    def p_to_far(x):
        return move(p_sum, p_far.at[chip], pf_send.at[x], pf_recv.at[chip], x * 2 + core)

    def p_from_far(x):
        return move(p_sum, p_far.at[x], pf_send.at[x], pf_recv.at[x], x * 2 + core)

    p_first = move(p_ref.at[1 - core], p_near, p_send.at[0], p_recv.at[0], partner)
    p_first.start()
    for x in range(chips):
        @pl.when(x < chip)
        def _():
            to_near(x).start()

    @pl.when(core == 1)
    def _():
        to_near(chip).start()

    for x in range(chips):
        @pl.when(x < chip)
        def _():
            to_near(x).wait_recv()
            total = g_ref[x * 2 + core].astype(jnp.float32) + near[x].astype(jnp.float32)
            sums[x] = total.astype(sums.dtype)
            to_far(x).start()

    p_first.wait_recv()
    p_sum[...] = p_ref[core] + p_near[...]
    for x in range(chips):
        @pl.when(x != chip)
        def _():
            p_to_far(x).start()
    p_out[core] = p_sum[...]
    for x in range(chips):
        @pl.when(x != chip)
        def _():
            p_from_far(x).wait_recv()
            p_out[core] += p_far[x]
    p_mine = move(p_out.at[core], p_out.at[core], p_send.at[1], p_recv.at[1], partner)
    p_theirs = move(p_out.at[core], p_out.at[1 - core], p_send.at[1], p_recv.at[1], partner)
    p_mine.start()

    @pl.when(core == 0)
    def _():
        to_near(chip).wait_recv()
    for x in range(chips):
        @pl.when(x > chip)
        def _():
            from_far(x).wait_recv()

    for which, out in ((0, k_out), (1, v_out)):
        mine = g_ref[me, which].astype(jnp.float32)
        mine += jnp.where(core == 0, near[chip, which].astype(jnp.float32), 0.0)
        for x in range(1, chips):
            mine += jnp.where(x > chip, far[x, which].astype(jnp.float32), 0.0)
        out[...] = mine.astype(out.dtype)

    p_first.wait_send()
    for x in range(chips):
        @pl.when(x < chip)
        def _():
            to_near(x).wait_send()
            to_far(x).wait_send()

        @pl.when(x != chip)
        def _():
            p_to_far(x).wait_send()

    @pl.when(core == 1)
    def _():
        to_near(chip).wait_send()
    p_mine.wait_send()
    p_theirs.wait_recv()


def reduce(gkv, gp):
    n = gkv.shape[0]
    chips = n // 2
    vmem = pl.BlockSpec(memory_space=pltpu.VMEM)
    piece = gkv.shape[1:]
    dma = pltpu.SemaphoreType.DMA
    return pl.pallas_call(
        functools.partial(reduce_kernel, n),
        in_specs=[vmem] * 2,
        out_specs=[vmem] * 3,
        out_shape=[
            jax.ShapeDtypeStruct(piece[1:], gkv.dtype),
            jax.ShapeDtypeStruct(piece[1:], gkv.dtype),
            jax.ShapeDtypeStruct(gp.shape, gp.dtype),
        ],
        scratch_shapes=[
            pltpu.VMEM((chips,) + piece, gkv.dtype),
            pltpu.VMEM((chips,) + piece, gkv.dtype),
            pltpu.VMEM((chips,) + piece, gkv.dtype),
            pltpu.VMEM(gp.shape[1:], gp.dtype),
            pltpu.VMEM(gp.shape[1:], gp.dtype),
            pltpu.VMEM((chips,) + gp.shape[1:], gp.dtype),
            dma((chips,)), dma((chips,)), dma((chips,)), dma((chips,)),
            dma((2,)), dma((2,)), dma((chips,)), dma((chips,)),
        ],
        compiler_params=pltpu.CompilerParams(
            collective_id=1, has_side_effects=True, vmem_limit_bytes=32 * 2**20
        ),
    )(gkv, gp)


def on_device(
    queries, seq_keys, seq_values, out_grad, prefix_keys, prefix_values,
    global_ids, rand_owner, rand_offset, doc_length,
):
    tokens, groups, width = seq_keys.shape
    shape = (tokens, groups, queries.shape[1] // groups, width)
    own = jnp.stack([seq_keys, seq_values]).transpose(0, 2, 1, 3)
    kv = gather(own, lax.axis_size("seq"))
    o, dq, gkv, gp = attend(
        queries.reshape(shape), out_grad.reshape(shape), kv,
        prefix_keys.transpose(1, 0, 2), prefix_values.transpose(1, 0, 2),
        global_ids, rand_owner, rand_offset, doc_length,
    )
    gk, gv, gp = reduce(gkv, gp)
    gk, gv = gk.transpose(1, 0, 2), gv.transpose(1, 0, 2)
    gp = gp.transpose(0, 2, 1, 3)
    return (o.reshape(queries.shape), dq.reshape(queries.shape), gk, gv, gp[0], gp[1])


def solution(mesh):
    tok = P(("groups", "seq"), "head", None)
    pre = P(None, "head", None)
    row = P(("groups", "seq"), None)
    out = P("groups", "head", None)
    return jax.shard_map(
        on_device,
        mesh=mesh,
        in_specs=(tok, tok, tok, tok, pre, pre, P("groups"), row, row, P("groups")),
        out_specs=(tok, tok, tok, tok, out, out),
        check_vma=False,
    )
```
